32 devices in a mesh: parts: 2 (over x), seq: 16 (over z, y, core).
Axes of the slice: x: 2, y: 2, z: 4, core: 2. Of those that a mesh axis runs over, the one named last changes fastest.
Arguments:
- inputs: bfloat16 [524288, 512], P(('parts', 'seq')), parts along dimension 0, may hold values from -6 to 6
- cotangent: bfloat16 [524288, 512], P(('parts', 'seq')), parts along dimension 0, may hold values from -6 to 6
- first_block: bfloat16 [512, 512], P('seq'), may hold values from -0.25 to 0.25
- second_block: bfloat16 [512, 512], P('seq'), may hold values from -0.25 to 0.25
- twiddle: float32 [512, 512], P('seq'), may hold values from 0.25 to 1.75
Outputs:
- grad_input: bfloat16 [524288, 512], P(('parts', 'seq')), parts along dimension 0
- grad_first: float32 [1024, 512], P(('parts', 'seq')), parts along dimension 0
- grad_second: float32 [1024, 512], P(('parts', 'seq')), parts along dimension 0
- grad_twiddle: float32 [1024, 512], P(('parts', 'seq')), parts along dimension 0
The draws below stay inside these ranges and needn't reach their ends.
There are 2 independent parts, one for each index of `parts`. The reference program is written for one: setup_inputs(seed, part) draws one part's arguments, and reference() takes and returns one part's arrays. A program takes and returns all parts, laid end to end along the dimension named above; an argument that names none is the same for every part. Nothing has to cross between parts.
All inputs are finite; a program needn't handle non-finite values.
Results may differ from the reference program's by a relative error of at most 0.0061.
Values may be sent and summed in bfloat16 or wider, within the bound.
A program may use at most 320 MiB of HBM per device.

```python
import jax
import jax.numpy as jnp

B = 512
C = 512
L = 262144


def shard_levels(own_key, dims, pieces, least, largest):
    factor_of = 1.0
    for dim, shards_of in pieces:
        draws = jax.random.uniform(jax.random.fold_in(jax.random.fold_in(own_key, 6), dim), (shards_of,), jnp.float32, least / len(pieces), largest / len(pieces))
        factor_of = factor_of * jnp.repeat(jnp.exp(draws), dims[dim] // shards_of).reshape((-1,) + (1,) * (len(dims) - 1 - dim))
    return factor_of


def centred(rng, extent, deviation, limit, pieces=(), dtype=jnp.bfloat16):
    loudness = shard_levels(rng, extent, pieces, -0.22, 0.18) if pieces else 1.0
    values = jax.random.normal(rng, extent, jnp.float32) * deviation * loudness
    return jnp.minimum(jnp.maximum(values, -limit), limit).astype(dtype)


def setup_inputs(seed: int = 0, part: int = 0) -> dict:
    keys = jax.random.split(jax.random.key(seed), 6)
    own_keys = jax.random.split(jax.random.fold_in(keys[5], part), 6)
    return {
        "inputs": centred(own_keys[0], (L, C), 1.0, 6.0, ((0, 16),)),
        "cotangent": centred(own_keys[1], (L, C), 1.0, 6.0, ((0, 16),)),
        "first_block": centred(keys[2], (B, B), B ** -0.5, 0.25, ((0, 16),)),
        "second_block": centred(keys[3], (B, B), B ** -0.5, 0.25, ((0, 16),)),
        "twiddle": jnp.clip(0.25 + 1.5 * jax.random.uniform(keys[4], (B, B), jnp.float32) ** shard_levels(keys[4], (B, B), ((0, 16),), -0.2, 0.2), 0.25, 1.75),
    }


def reference(inputs, cotangent, first_block, second_block, twiddle):
    f32 = jnp.float32
    xval = inputs.reshape(B, B, C).astype(f32)
    dyval = cotangent.reshape(B, B, C).astype(f32)
    block_one = first_block.astype(f32)
    block_two = second_block.astype(f32)
    tw_cols = twiddle.T[:, :, None]
    mixed_one = jnp.einsum("jk,ikc->ijc", block_one, xval).astype(jnp.bfloat16)
    scaled = (tw_cols * mixed_one.astype(f32)).astype(jnp.bfloat16)
    gated_mix = jnp.einsum("ik,kjc->ijc", block_two, scaled.astype(f32)).astype(jnp.bfloat16)
    grad_mix = (dyval * xval).astype(jnp.bfloat16)
    back_two = jnp.einsum("ki,kjc->ijc", block_two, grad_mix.astype(f32))
    grad_twiddle = jnp.sum(back_two * mixed_one.astype(f32), axis=2).T / (C ** 0.5)
    back_one = (tw_cols * back_two).astype(jnp.bfloat16)
    grad_second = jnp.einsum("ijc,kjc->ik", grad_mix.astype(f32), scaled.astype(f32)) / C
    grad_first = jnp.einsum("ijc,ikc->jk", back_one.astype(f32), xval) / C
    total = dyval * gated_mix.astype(f32) + jnp.einsum("jk,ijc->ikc", block_one, back_one.astype(f32))
    grad_input = total.astype(jnp.bfloat16).reshape(B * B, C)
    return grad_input, grad_first, grad_second, grad_twiddle
```

```python
import jax
import jax.numpy as jnp
from jax import lax
from jax.experimental import pallas as pl
from jax.experimental.pallas import tpu as pltpu
from jax.sharding import PartitionSpec as P

F32 = jnp.float32
BF16 = jnp.bfloat16
LANES = 128


def channel_kernel(
    x_ref, dy_ref, f_ref, ft_ref, s_ref, st_ref, tw_ref, gf_in, gs_in, gt_in,
    gi_ref, gf_ref, gs_ref, gt_ref,
):
    @pl.when(pl.program_id(0) == 0)
    def _():
        gf_ref[...] = gf_in[...]
        gs_ref[...] = gs_in[...]
        gt_ref[...] = gt_in[...]

    order = f_ref.shape[0]
    xf = x_ref[...].astype(F32).reshape(order, order)
    dyf = dy_ref[...].astype(F32).reshape(order, order)
    xb = xf.astype(BF16)
    tw = tw_ref[...]
    m1 = jnp.dot(xb, ft_ref[...], preferred_element_type=F32).astype(BF16).astype(F32)
    scaled = (tw * m1).astype(BF16)
    grad_mix = (dyf * xf).astype(BF16)
    gated = jnp.dot(s_ref[...], scaled, preferred_element_type=F32).astype(BF16)
    back_two = jnp.dot(st_ref[...], grad_mix, preferred_element_type=F32)
    gt_ref[...] += back_two * m1
    back_one = (tw * back_two).astype(BF16)
    gs_ref[...] += lax.dot_general(
        grad_mix, scaled, (((1,), (1,)), ((), ())), preferred_element_type=F32
    )
    gf_ref[...] += lax.dot_general(
        back_one, xb, (((0,), (0,)), ((), ())), preferred_element_type=F32
    )
    gi = dyf * gated.astype(F32) + jnp.dot(back_one, f_ref[...], preferred_element_type=F32)
    gi_ref[...] = gi.reshape(gi_ref.shape).astype(BF16)


def channels_call(xc, dyc, f, ft, s, st, tw, grads):
    devices, own, rows, order = xc.shape
    block = pl.BlockSpec((devices, None, rows, order), lambda c: (0, c, 0, 0))
    square = pl.BlockSpec((order, order), lambda c: (0, 0))
    total = jax.ShapeDtypeStruct((order, order), F32)
    gi, *grads = pl.pallas_call(
        channel_kernel,
        grid=(own,),
        out_shape=(jax.ShapeDtypeStruct(xc.shape, BF16), total, total, total),
        in_specs=[block] * 2 + [square] * 8,
        out_specs=(block, square, square, square),
        compiler_params=pltpu.CompilerParams(vmem_limit_bytes=56 * 1024 * 1024),
        cost_estimate=pl.CostEstimate(
            flops=12 * own * order**3,
            bytes_accessed=6 * own * order**2 + 30 * order**2,
            transcendentals=0,
        ),
    )(xc, dyc, f, ft, s, st, tw, *grads)
    return gi, tuple(grads)


def to_channels_kernel(x_ref, o_ref, held):
    count = x_ref.shape[0]
    lanes = x_ref.shape[2]
    for i in range(count):
        for q in range(x_ref.shape[1] // LANES):
            square = x_ref[i, pl.ds(q * LANES, LANES), :].astype(F32).T
            held[pl.ds(q * lanes * count + i, lanes, stride=count), :] = square
    for q in range(x_ref.shape[1] // LANES):
        piece = held[pl.ds(q * lanes * count, lanes * count), :]
        o_ref[:, :, pl.ds(q * LANES, LANES)] = piece.reshape(lanes, count, LANES).astype(BF16)


def to_channels(array, at, chunk):
    rows, order, _ = array.shape
    count = min(rows, 16)
    return pl.pallas_call(
        to_channels_kernel,
        grid=(chunk // LANES, rows // count),
        out_shape=jax.ShapeDtypeStruct((chunk, rows, order), BF16),
        in_specs=[pl.BlockSpec((count, order, LANES), lambda c, i: (i, 0, at // LANES + c))],
        out_specs=pl.BlockSpec((LANES, count, order), lambda c, i: (c, i, 0)),
        scratch_shapes=[pltpu.VMEM((count * order, LANES), F32)],
        compiler_params=pltpu.CompilerParams(vmem_limit_bytes=56 * 1024 * 1024),
        cost_estimate=pl.CostEstimate(
            flops=0, bytes_accessed=4 * chunk * rows * order, transcendentals=0
        ),
    )(array)


def to_positions_kernel(b_ref, *refs):
    o_ref, held = refs[-2:]
    count = o_ref.shape[0]
    lanes = o_ref.shape[2]
    for q in range(o_ref.shape[1] // LANES):
        piece = b_ref[:, :, pl.ds(q * LANES, LANES)].astype(F32)
        held[pl.ds(q * lanes * count, lanes * count), :] = piece.reshape(lanes * count, LANES)
    for i in range(count):
        for q in range(o_ref.shape[1] // LANES):
            square = held[pl.ds(q * lanes * count + i, lanes, stride=count), :].T
            o_ref[i, pl.ds(q * LANES, LANES), :] = square.astype(BF16)


def to_positions(back, at, channels, result):
    chunk, rows, order = back.shape
    count = min(rows, 16)
    return pl.pallas_call(
        to_positions_kernel,
        grid=(chunk // LANES, rows // count),
        out_shape=jax.ShapeDtypeStruct((rows, order, channels), BF16),
        in_specs=[pl.BlockSpec((LANES, count, order), lambda c, i: (c, i, 0))]
        + [pl.BlockSpec(memory_space=pl.ANY)] * len(result),
        out_specs=pl.BlockSpec((count, order, LANES), lambda c, i: (i, 0, at // LANES + c)),
        scratch_shapes=[pltpu.VMEM((count * order, LANES), F32)],
        input_output_aliases={1: 0} if result else {},
        compiler_params=pltpu.CompilerParams(vmem_limit_bytes=56 * 1024 * 1024),
        cost_estimate=pl.CostEstimate(
            flops=0, bytes_accessed=4 * chunk * rows * order, transcendentals=0
        ),
    )(back, *result)


def on_device(inputs, cotangent, first_block, second_block, twiddle):
    channels = inputs.shape[1]
    rows, order = first_block.shape
    devices = order // rows
    chunk = channels // 2
    own = chunk // devices
    xval = inputs.reshape(rows, order, channels)
    dyval = cotangent.reshape(rows, order, channels)

    def send(array, at):
        part = to_channels(array, at, chunk).reshape(devices, own, rows, order)
        return lax.all_to_all(part, "seq", split_axis=0, concat_axis=0)

    small = jnp.stack([first_block.astype(F32), second_block.astype(F32), twiddle])
    small = lax.all_gather(small, "seq", axis=0)
    small = small.transpose(1, 0, 2, 3).reshape(3, order, order)
    f, s = small[0].astype(BF16), small[1].astype(BF16)
    ft, st, tw = f.T, s.T, small[2].T

    zero = jnp.zeros((order, order), F32)
    grads = (zero, zero, zero)
    result = ()
    for at in range(0, channels, chunk):
        gi, grads = channels_call(send(xval, at), send(dyval, at), f, ft, s, st, tw, grads)
        back = lax.all_to_all(gi, "seq", split_axis=0, concat_axis=0)
        result = (to_positions(back.reshape(chunk, rows, order), at, channels, result),)

    first, second, tw_grad = grads
    terms = jnp.stack([first, second, tw_grad.T]).reshape(3, devices, rows, order)
    terms = terms.transpose(1, 0, 2, 3).reshape(3 * order, order)
    terms = lax.psum_scatter(terms, "seq", scatter_dimension=0, tiled=True)
    terms = terms.reshape(3, rows, order)
    grad_first = terms[0] / channels
    grad_second = terms[1] / channels
    grad_twiddle = terms[2] / channels**0.5
    return (result[0].reshape(rows * order, channels), grad_first, grad_second, grad_twiddle)


def solution(mesh):
    in_specs = (
        P(("parts", "seq"), None),
        P(("parts", "seq"), None),
        P("seq", None),
        P("seq", None),
        P("seq", None),
    )
    out_specs = (
        P(("parts", "seq"), None),
        P(("parts", "seq"), None),
        P(("parts", "seq"), None),
        P(("parts", "seq"), None),
    )
    return jax.shard_map(
        on_device, mesh=mesh, in_specs=in_specs, out_specs=out_specs, check_vma=False
    )
```

```python
import jax
import jax.numpy as jnp
from jax import lax
from jax.experimental import pallas as pl
from jax.experimental.pallas import tpu as pltpu
from jax.sharding import PartitionSpec as P

F32 = jnp.float32
BF16 = jnp.bfloat16
LANES = 128


def channel_kernel(
    x_ref, dy_ref, f_ref, ft_ref, s_ref, st_ref, tw_ref, gf_in, gs_in, gt_in,
    gi_ref, gf_ref, gs_ref, gt_ref,
):
    @pl.when(pl.program_id(0) == 0)
    def _():
        gf_ref[...] = gf_in[...]
        gs_ref[...] = gs_in[...]
        gt_ref[...] = gt_in[...]

    order = f_ref.shape[0]
    xf = x_ref[...].astype(F32).reshape(order, order)
    dyf = dy_ref[...].astype(F32).reshape(order, order)
    xb = xf.astype(BF16)
    tw = tw_ref[...]
    m1 = jnp.dot(xb, ft_ref[...], preferred_element_type=F32).astype(BF16).astype(F32)
    scaled = (tw * m1).astype(BF16)
    grad_mix = (dyf * xf).astype(BF16)
    gated = jnp.dot(s_ref[...], scaled, preferred_element_type=F32).astype(BF16)
    back_two = jnp.dot(st_ref[...], grad_mix, preferred_element_type=F32)
    gt_ref[...] += back_two * m1
    back_one = (tw * back_two).astype(BF16)
    gs_ref[...] += lax.dot_general(
        grad_mix, scaled, (((1,), (1,)), ((), ())), preferred_element_type=F32
    )
    gf_ref[...] += lax.dot_general(
        back_one, xb, (((0,), (0,)), ((), ())), preferred_element_type=F32
    )
    gi = dyf * gated.astype(F32) + jnp.dot(back_one, f_ref[...], preferred_element_type=F32)
    gi_ref[...] = gi.reshape(gi_ref.shape).astype(BF16)


def channels_call(xc, dyc, f, ft, s, st, tw, grads):
    devices, own, rows, order = xc.shape
    block = pl.BlockSpec((devices, None, rows, order), lambda c: (0, c, 0, 0))
    square = pl.BlockSpec((order, order), lambda c: (0, 0))
    total = jax.ShapeDtypeStruct((order, order), F32)
    gi, *grads = pl.pallas_call(
        channel_kernel,
        grid=(own,),
        out_shape=(jax.ShapeDtypeStruct(xc.shape, BF16), total, total, total),
        in_specs=[block] * 2 + [square] * 8,
        out_specs=(block, square, square, square),
        compiler_params=pltpu.CompilerParams(vmem_limit_bytes=56 * 1024 * 1024),
        cost_estimate=pl.CostEstimate(
            flops=12 * own * order**3,
            bytes_accessed=6 * own * order**2 + 30 * order**2,
            transcendentals=0,
        ),
    )(xc, dyc, f, ft, s, st, tw, *grads)
    return gi, tuple(grads)


def to_channels_kernel(x_ref, *refs):
    o_ref, held = refs[-2:]
    count = x_ref.shape[0]
    lanes = x_ref.shape[2]
    for i in range(count):
        for q in range(x_ref.shape[1] // LANES):
            square = x_ref[i, pl.ds(q * LANES, LANES), :].astype(F32).T
            held[pl.ds(q * lanes * count + i, lanes, stride=count), :] = square
    for q in range(x_ref.shape[1] // LANES):
        piece = held[pl.ds(q * lanes * count, lanes * count), :]
        o_ref[:, :, pl.ds(q * LANES, LANES)] = piece.reshape(lanes, count, LANES).astype(BF16)


def to_channels(array, at, chunk, after):
    rows, order, _ = array.shape
    count = min(rows, 16)
    return pl.pallas_call(
        to_channels_kernel,
        grid=(chunk // LANES, rows // count),
        out_shape=jax.ShapeDtypeStruct((chunk, rows, order), BF16),
        in_specs=[pl.BlockSpec((count, order, LANES), lambda c, i: (i, 0, at // LANES + c))]
        + [pl.BlockSpec(memory_space=pl.ANY)] * len(after),
        out_specs=pl.BlockSpec((LANES, count, order), lambda c, i: (c, i, 0)),
        scratch_shapes=[pltpu.VMEM((count * order, LANES), F32)],
        compiler_params=pltpu.CompilerParams(vmem_limit_bytes=56 * 1024 * 1024),
        cost_estimate=pl.CostEstimate(
            flops=0, bytes_accessed=4 * chunk * rows * order, transcendentals=0
        ),
    )(array, *after)


def to_positions_kernel(b_ref, *refs):
    o_ref, held = refs[-2:]
    count = o_ref.shape[0]
    lanes = o_ref.shape[2]
    for q in range(o_ref.shape[1] // LANES):
        piece = b_ref[:, :, pl.ds(q * LANES, LANES)].astype(F32)
        held[pl.ds(q * lanes * count, lanes * count), :] = piece.reshape(lanes * count, LANES)
    for i in range(count):
        for q in range(o_ref.shape[1] // LANES):
            square = held[pl.ds(q * lanes * count + i, lanes, stride=count), :].T
            o_ref[i, pl.ds(q * LANES, LANES), :] = square.astype(BF16)


def to_positions(back, at, channels, result):
    chunk, rows, order = back.shape
    count = min(rows, 16)
    return pl.pallas_call(
        to_positions_kernel,
        grid=(chunk // LANES, rows // count),
        out_shape=jax.ShapeDtypeStruct((rows, order, channels), BF16),
        in_specs=[pl.BlockSpec((LANES, count, order), lambda c, i: (c, i, 0))]
        + [pl.BlockSpec(memory_space=pl.ANY)] * len(result),
        out_specs=pl.BlockSpec((count, order, LANES), lambda c, i: (i, 0, at // LANES + c)),
        scratch_shapes=[pltpu.VMEM((count * order, LANES), F32)],
        input_output_aliases={1: 0} if result else {},
        compiler_params=pltpu.CompilerParams(vmem_limit_bytes=56 * 1024 * 1024),
        cost_estimate=pl.CostEstimate(
            flops=0, bytes_accessed=4 * chunk * rows * order, transcendentals=0
        ),
    )(back, *result)


def on_device(inputs, cotangent, first_block, second_block, twiddle):
    channels = inputs.shape[1]
    rows, order = first_block.shape
    devices = order // rows
    chunk = channels // 2
    own = chunk // devices
    xval = inputs.reshape(rows, order, channels)
    dyval = cotangent.reshape(rows, order, channels)

    def send(array, at, *after):
        part = to_channels(array, at, chunk, after).reshape(devices, own, rows, order)
        return lax.all_to_all(part, "seq", split_axis=0, concat_axis=0)

    small = jnp.stack([first_block.astype(F32), second_block.astype(F32), twiddle])
    small = lax.all_gather(small, "seq", axis=0)
    small = small.transpose(1, 0, 2, 3).reshape(3, order, order)
    f, s = small[0].astype(BF16), small[1].astype(BF16)
    ft, st, tw = f.T, s.T, small[2].T

    zero = jnp.zeros((order, order), F32)
    grads = (zero, zero, zero)
    result = ()
    before = small
    for at in range(0, channels, chunk):
        xc, dyc = send(xval, at), send(dyval, at, before)
        gi, grads = channels_call(xc, dyc, f, ft, s, st, tw, grads)
        before = gi
        back = lax.all_to_all(gi, "seq", split_axis=0, concat_axis=0)
        result = (to_positions(back.reshape(chunk, rows, order), at, channels, result),)

    first, second, tw_grad = grads
    terms = jnp.stack([first, second, tw_grad.T]).reshape(3, devices, rows, order)
    terms = terms.transpose(1, 0, 2, 3).reshape(3 * order, order)
    terms = lax.psum_scatter(terms, "seq", scatter_dimension=0, tiled=True)
    terms = terms.reshape(3, rows, order)
    grad_first = terms[0] / channels
    grad_second = terms[1] / channels
    grad_twiddle = terms[2] / channels**0.5
    return (result[0].reshape(rows * order, channels), grad_first, grad_second, grad_twiddle)


def solution(mesh):
    in_specs = (
        P(("parts", "seq"), None),
        P(("parts", "seq"), None),
        P("seq", None),
        P("seq", None),
        P("seq", None),
    )
    out_specs = (
        P(("parts", "seq"), None),
        P(("parts", "seq"), None),
        P(("parts", "seq"), None),
        P(("parts", "seq"), None),
    )
    return jax.shard_map(
        on_device, mesh=mesh, in_specs=in_specs, out_specs=out_specs, check_vma=False
    )
```
